32 devices in a mesh: fsdp: 16 (over z, y, x), tensor: 2 (over core).
Axes of the slice: x: 2, y: 2, z: 4, core: 2. Of those that a mesh axis runs over, the one named last changes fastest.
Arguments:
- tokens: bfloat16 [16384, 1024], P('fsdp'), may hold values from -6 to 6
- lengths: int32 [16, 8], P('fsdp'), may hold values from 1 to 512, 1024 in all within a row
- w_query: bfloat16 [1024, 1024], P('fsdp', 'tensor'), may hold values from -0.1875 to 0.1875
- key_weight: bfloat16 [1024, 512], P('fsdp', 'tensor'), may hold values from -0.1875 to 0.1875
- value_weight: bfloat16 [1024, 512], P('fsdp', 'tensor'), may hold values from -0.1875 to 0.1875
- w_output: bfloat16 [1024, 1024], P('tensor', 'fsdp'), may hold values from -1.5 to 1.5
- w_gate: bfloat16 [1024, 4608], P('fsdp', 'tensor'), may hold values from -0.1875 to 0.1875
- w_up: bfloat16 [1024, 4608], P('fsdp', 'tensor'), may hold values from -0.1875 to 0.1875
- w_down: bfloat16 [4608, 1024], P('tensor', 'fsdp'), may hold values from -0.09375 to 0.09375
- gain_attn: bfloat16 [1024], P('fsdp'), may hold values from 0.099609375 to 1.8984375
- gain_ffn: bfloat16 [1024], P('fsdp'), may hold values from 0.099609375 to 1.8984375
- gain_query: bfloat16 [64], replicated, may hold values from 0.099609375 to 1.8984375
- key_norm_gain: bfloat16 [64], replicated, may hold values from 0.099609375 to 1.8984375
- cotangent: bfloat16 [16384, 1024], P('fsdp'), may hold values from -6 to 6
Outputs:
- layer_out: bfloat16 [16384, 1024], P('fsdp')
- token_grad: bfloat16 [16384, 1024], P('fsdp')
- grad_query: float32 [1024, 1024], P('fsdp', 'tensor')
- grad_key: float32 [1024, 512], P('fsdp', 'tensor')
- grad_value: float32 [1024, 512], P('fsdp', 'tensor')
- grad_output: float32 [1024, 1024], P('tensor', 'fsdp')
- grad_gate: float32 [1024, 4608], P('fsdp', 'tensor')
- grad_up: float32 [1024, 4608], P('fsdp', 'tensor')
- grad_down: float32 [4608, 1024], P('tensor', 'fsdp')
- grad_gain_attn: float32 [1024], P('fsdp')
- grad_gain_ffn: float32 [1024], P('fsdp')
- grad_gain_query: float32 [64], replicated
- grad_gain_key: float32 [64], replicated
The draws below stay inside these ranges and needn't reach their ends.
Inputs may be any that keep to these rules, and one draw needn't show every extreme that they name: Each lengths row sums to 1024 and holds one length of exactly 512.
All inputs are finite; a program needn't handle non-finite values.
Results may differ from the reference program's by a relative error of at most 0.014.
Values may be sent and summed in bfloat16 or wider, within the bound.
A program may use at most 192 MiB of HBM per device.

```python
import math
import jax
import jax.numpy as jnp
import numpy as np
from jax import lax

MODEL_WIDTH = 1024
HQ = 16
KEY_VALUE_HEADS = 8
HEAD_SIZE = 64
FF = 4608
TOKENS_PER_SHARD = 1024
MAXLEN = 512
SEQS_DEV = 8
QUERY_GROUP = 2
QUERY_BLOCK_ROWS = 512
TOKENS = 16384
N_FSDP = 16


def with_spikes(drawn, rng, source, target, blocks, factor):
    def block_of(dim):
        return (jnp.arange(drawn.shape[dim]) // (drawn.shape[dim] // blocks)).reshape((-1,) + (1,) * (drawn.ndim - 1 - dim))

    one_side = jax.random.permutation(rng, blocks)[block_of(target)]
    far = (block_of(target) + blocks // 2) % blocks
    return jnp.where((block_of(source) == one_side) | (block_of(source) == far), factor * drawn, drawn)


def level_of(rng, extent, shards, least, largest):
    factor_of, own = 1.0, jax.random.fold_in(rng, 6)
    for dim, blocks in shards:
        draws = jnp.exp(jax.random.uniform(jax.random.fold_in(own, dim), (blocks,), jnp.float32, least / len(shards), largest / len(shards)))
        factor_of = factor_of * jnp.repeat(draws, extent[dim] // blocks).reshape([-1 if axis == dim else 1 for axis in range(len(extent))])
    return factor_of


def split_up(number_of, total, most, slope):
    weights = [(1 << 20) // math.isqrt(grade ** slope) + 1 for grade in range(2, number_of + 1)]
    rest, holding = total - most - (number_of - 1), [1] * (number_of - 1)
    while rest > 0:
        movable = [i for i in range(number_of - 1) if holding[i] < most]
        whole, remaining = sum([weights[i] for i in movable]), rest
        for i in movable:
            extra = min(most - holding[i], max(1, remaining * weights[i] // whole), rest)
            holding[i] = holding[i] + extra
            rest = rest - extra
    return np.array([most] + holding)


def uneven(rng, amount, total, reach, lean):
    if amount == 2:
        one = jax.random.randint(rng, (), max(1, total - reach), min(reach, total - 1) + 1)
        return jnp.stack([one, total - one])
    sizes = jnp.asarray(split_up(amount, total, reach, lean), jnp.int32)
    pairs = (amount - 1) // 2
    donor, receiver = sizes[1:1 + 2 * pairs:2], sizes[2:2 + 2 * pairs:2]
    room = jnp.minimum(donor - 1, reach - receiver)
    shifted = jax.random.randint(jax.random.fold_in(rng, 1), (pairs,), 0, 1 << 20) % (room + 1)
    sizes = sizes.at[1:1 + 2 * pairs:2].set(donor - shifted).at[2:2 + 2 * pairs:2].set(receiver + shifted)
    return sizes[jax.random.permutation(jax.random.fold_in(rng, 2), amount)]


def gaussian(own_key, dims, scale, bound, pieces=(), held_as=jnp.bfloat16):
    loudness = level_of(own_key, dims, pieces, -0.22, 0.18) if pieces else 1.0
    entries = jax.random.normal(own_key, dims, jnp.float32) * scale * loudness
    return jnp.minimum(jnp.maximum(entries, -bound), bound).astype(held_as)


def heavy_noise(key, extent, scale, reach, pieces, heavy, kind=jnp.bfloat16):
    drawn = scale * jax.random.normal(key, extent, jnp.float32)
    if pieces:
        drawn = drawn * level_of(key, extent, pieces, -0.22, 0.18)
    return jnp.clip(with_spikes(drawn, jax.random.fold_in(key, 3), *heavy), -reach, reach).astype(kind)


def setup_inputs(seed: int = 0) -> dict:
    key_of = jax.random.split(jax.random.key(seed), 15)
    return {
        "tokens": heavy_noise(key_of[0], (TOKENS, MODEL_WIDTH), 1.0, 6.0, ((0, 16),), (0, 1, 16, 2.0)),
        "lengths": jax.vmap(lambda own: uneven(own, SEQS_DEV, TOKENS_PER_SHARD, MAXLEN, 2))(jax.random.split(key_of[1], N_FSDP)).reshape((N_FSDP, SEQS_DEV)).astype(jnp.int32),
        "w_query": gaussian(key_of[2], (MODEL_WIDTH, HQ * HEAD_SIZE), MODEL_WIDTH ** -0.5, 0.1875, ((0, 16), (1, 2))),
        "key_weight": gaussian(key_of[3], (MODEL_WIDTH, KEY_VALUE_HEADS * HEAD_SIZE), MODEL_WIDTH ** -0.5, 0.1875, ((0, 16), (1, 2))),
        "value_weight": gaussian(key_of[4], (MODEL_WIDTH, KEY_VALUE_HEADS * HEAD_SIZE), MODEL_WIDTH ** -0.5, 0.1875, ((0, 16), (1, 2))),
        "w_output": gaussian(key_of[5], (HQ * HEAD_SIZE, MODEL_WIDTH), (MODEL_WIDTH // 64) ** -0.5, 1.5, ((0, 2), (1, 16))),
        "w_gate": gaussian(key_of[6], (MODEL_WIDTH, FF), MODEL_WIDTH ** -0.5, 0.1875, ((0, 16), (1, 2))),
        "w_up": gaussian(key_of[7], (MODEL_WIDTH, FF), MODEL_WIDTH ** -0.5, 0.1875, ((0, 16), (1, 2))),
        "w_down": gaussian(key_of[8], (FF, MODEL_WIDTH), FF ** -0.5, 0.09375, ((0, 2), (1, 16))),
        "gain_attn": jnp.clip(1.0 + 0.18 * jax.random.normal(key_of[9], (MODEL_WIDTH,), jnp.float32), 0.099609375, 1.8984375).astype(jnp.bfloat16),
        "gain_ffn": jnp.clip(1.0 + 0.18 * jax.random.normal(key_of[10], (MODEL_WIDTH,), jnp.float32), 0.099609375, 1.8984375).astype(jnp.bfloat16),
        "gain_query": jnp.clip(1.0 + 0.18 * jax.random.normal(key_of[11], (HEAD_SIZE,), jnp.float32), 0.099609375, 1.8984375).astype(jnp.bfloat16),
        "key_norm_gain": jnp.clip(1.0 + 0.18 * jax.random.normal(key_of[12], (HEAD_SIZE,), jnp.float32), 0.099609375, 1.8984375).astype(jnp.bfloat16),
        "cotangent": heavy_noise(key_of[13], (TOKENS, MODEL_WIDTH), 1.0, 6.0, ((0, 16),), (0, 1, 16, 2.0)),
    }


EPS = 1e-05
THETA = 1000000.0

@jax.custom_vjp
def lower_precision(v):
    return lax.optimization_barrier(v.astype(jnp.bfloat16)).astype(jnp.float32)

@jax.custom_vjp
def lower_precision_backward(v):
    return v

def low_keep(v):
    return (lower_precision(v), None)

def low_pass(kept, grad):
    return (grad,)

def back_keep(v):
    return (v, None)

def back_low(kept, grad):
    return (lower_precision(grad),)
lower_precision.defvjp(low_keep, low_pass)
lower_precision_backward.defvjp(back_keep, back_low)

def matrix_product(left, right):
    return jnp.dot(left, right, precision=lax.Precision.HIGHEST, preferred_element_type=jnp.float32)

def root_mean_scale(value, gain):
    return value * lax.rsqrt(lax.optimization_barrier(jnp.mean(value * value, axis=-1, keepdims=True)) + EPS) * gain

def apply_rotary(value, cosine_table, sine_table):
    half = value.shape[-1] // 2
    first = value[..., :half]
    second = value[..., half:]
    return jnp.concatenate([first * cosine_table - second * sine_table, second * cosine_table + first * sine_table], axis=-1)

def attention(query_rounded_copy, key_rounded_copy, value_rounded_copy, segment):
    scale = HEAD_SIZE ** (-0.5)
    rows_all = jnp.arange(TOKENS_PER_SHARD, dtype=jnp.int32)
    key_rows = key_rounded_copy.reshape(TOKENS_PER_SHARD, KEY_VALUE_HEADS, HEAD_SIZE)
    value_rows = value_rounded_copy.reshape(TOKENS_PER_SHARD, KEY_VALUE_HEADS, HEAD_SIZE)

    def block(start_offset):
        query_block_slice = lax.dynamic_slice_in_dim(query_rounded_copy, start_offset, QUERY_BLOCK_ROWS, 0).reshape(QUERY_BLOCK_ROWS, KEY_VALUE_HEADS, QUERY_GROUP, HEAD_SIZE)
        scores = jnp.einsum('bkgd,skd->kgbs', query_block_slice, key_rows, precision=lax.Precision.HIGHEST) * scale
        scores = lower_precision_backward(scores)
        rows = start_offset + jnp.arange(QUERY_BLOCK_ROWS, dtype=jnp.int32)
        seg_rows = lax.dynamic_slice_in_dim(segment, start_offset, QUERY_BLOCK_ROWS, 0)
        allowed = (seg_rows[:, None] == segment[None, :]) & (rows_all[None, :] <= rows[:, None])
        scores = jnp.where(allowed, scores, -1e+30)
        top = lax.optimization_barrier(jnp.max(scores, axis=-1, keepdims=True))
        weights = jnp.exp(scores - top)
        prob = lower_precision(weights / lax.optimization_barrier(jnp.sum(weights, axis=-1, keepdims=True)))
        return jnp.einsum('kgbs,skd->bkgd', prob, value_rows, precision=lax.Precision.HIGHEST).reshape(QUERY_BLOCK_ROWS, HQ * HEAD_SIZE)
    starts = jnp.arange(TOKENS_PER_SHARD // QUERY_BLOCK_ROWS, dtype=jnp.int32) * QUERY_BLOCK_ROWS
    return lax.map(jax.checkpoint(block), starts).reshape(TOKENS_PER_SHARD, HQ * HEAD_SIZE)

def block_rows(params, rows_in, lens):
    w_query, key_weight, value_weight, w_output, w_gate, w_up, w_down, gain_attn, gain_ffn, gain_query, key_norm_gain = params
    row_ids = jnp.arange(TOKENS_PER_SHARD, dtype=jnp.int32)
    ends = jnp.cumsum(lens)
    passed = row_ids[:, None] >= ends[None, :]
    segment = lax.optimization_barrier(jnp.sum(passed.astype(jnp.int32), axis=1))
    begin = lax.optimization_barrier(jnp.sum(jnp.where(passed, lens[None, :], 0), axis=1))
    position = (row_ids - begin).astype(jnp.float32)
    freq = THETA ** (-jnp.arange(HEAD_SIZE // 2, dtype=jnp.float32) * 2.0 / HEAD_SIZE)
    angle = position[:, None] * freq[None, :]
    cosine_table = jnp.cos(angle)[:, None, :]
    sine_table = jnp.sin(angle)[:, None, :]
    first_hidden = lower_precision(root_mean_scale(rows_in, gain_attn))
    q_raw = lower_precision_backward(matrix_product(first_hidden, w_query)).reshape(TOKENS_PER_SHARD, HQ, HEAD_SIZE)
    key_unnormed = lower_precision_backward(matrix_product(first_hidden, key_weight)).reshape(TOKENS_PER_SHARD, KEY_VALUE_HEADS, HEAD_SIZE)
    value = lower_precision(lower_precision_backward(matrix_product(first_hidden, value_weight)))
    query = lower_precision(apply_rotary(root_mean_scale(q_raw, gain_query), cosine_table, sine_table)).reshape(TOKENS_PER_SHARD, HQ * HEAD_SIZE)
    key = lower_precision(apply_rotary(root_mean_scale(key_unnormed, key_norm_gain), cosine_table, sine_table)).reshape(TOKENS_PER_SHARD, KEY_VALUE_HEADS * HEAD_SIZE)
    attended = lower_precision(lower_precision_backward(attention(query, key, value, segment)))
    branch = lower_precision_backward(matrix_product(attended, w_output))
    resid = rows_in + branch
    h_second = lower_precision(root_mean_scale(resid, gain_ffn))
    gate = lower_precision_backward(matrix_product(h_second, w_gate))
    upward = lower_precision_backward(matrix_product(h_second, w_up))
    hidden = lower_precision(gate * jax.nn.sigmoid(gate) * upward)
    return resid + lower_precision_backward(matrix_product(hidden, w_down))

def forward(params, rows_all, lengths):
    grouped = rows_all.reshape(N_FSDP, TOKENS_PER_SHARD, MODEL_WIDTH)

    def step(carry, pair):
        return (carry, block_rows(params, pair[0], pair[1]))
    _, outs = lax.scan(step, jnp.zeros((), jnp.float32), (grouped, lengths))
    return outs.reshape(TOKENS, MODEL_WIDTH)

def reference(tokens, lengths, w_query, key_weight, value_weight, w_output, w_gate, w_up, w_down, gain_attn, gain_ffn, gain_query, key_norm_gain, cotangent):
    params = tuple((p.astype(jnp.float32) for p in (w_query, key_weight, value_weight, w_output, w_gate, w_up, w_down, gain_attn, gain_ffn, gain_query, key_norm_gain)))
    rows_all = tokens.astype(jnp.float32)
    result, pull = jax.vjp(lambda p, r: forward(p, r, lengths), params, rows_all)
    grads, token_grad = pull(cotangent.astype(jnp.float32))
    return (result.astype(jnp.bfloat16), token_grad.astype(jnp.bfloat16), grads[0], grads[1], grads[2], grads[3], grads[4], grads[5], grads[6], grads[7], grads[8], grads[9], grads[10])
```

```python
import functools

import jax
import jax.numpy as jnp
from jax import lax
from jax.experimental import pallas as pl
from jax.experimental.pallas import tpu as pltpu
from jax.sharding import PartitionSpec as P

HEAD_SIZE = 64
HALF = 32
QUERY_GROUP = 2
BLOCK = 256
MAXLEN = 512
EPS = 1e-05
THETA = 1000000.0
PAIR = 2
VMEM = 60 * 1024 * 1024


def root_mean_scale(value, gain):
    return value * lax.rsqrt(jnp.mean(value * value, axis=-1, keepdims=True) + EPS) * gain


def swish_product(gate, upward):
    return gate * jax.nn.sigmoid(gate) * upward


def matrix_product(left, right):
    return jnp.dot(left, right, preferred_element_type=jnp.float32)


def matmul_t(left, right):
    return lax.dot_general(
        left, right, (((1,), (1,)), ((), ())), preferred_element_type=jnp.float32
    )


def inner_rows(left, right):
    return lax.dot_general(
        left, right, (((0,), (0,)), ((), ())), preferred_element_type=jnp.float32
    )


def swap_halves(value):
    return jnp.concatenate([value[:, HALF:], value[:, :HALF]], axis=1)


def head(index):
    return slice(index * HEAD_SIZE, (index + 1) * HEAD_SIZE)


def normed_rotated(raw, gain, cosine, sine):
    n = raw * lax.rsqrt(jnp.mean(raw * raw, axis=-1, keepdims=True) + EPS) * gain
    return (n * cosine + swap_halves(n) * sine).astype(jnp.bfloat16)


def undo_norm(raw, gain, cosine, sine, d_out):
    d_n = d_out * cosine - swap_halves(d_out) * sine
    r = lax.rsqrt(jnp.mean(raw * raw, axis=-1, keepdims=True) + EPS)
    scaled = raw * r
    d_gain = jnp.sum(d_n * scaled, axis=0, keepdims=True)
    g_d = gain * d_n
    d_raw = r * (g_d - scaled * jnp.mean(g_d * scaled, axis=-1, keepdims=True))
    return d_raw.astype(jnp.bfloat16), d_gain


def probabilities(query, key, begin, row0, key0):
    scores = matmul_t(query, key) * (HEAD_SIZE ** -0.5)
    rows = row0 + lax.broadcasted_iota(jnp.int32, scores.shape, 0)
    cols = key0 + lax.broadcasted_iota(jnp.int32, scores.shape, 1)
    allowed = (cols <= rows) & (cols >= begin)
    scores = jnp.where(allowed, scores, -1e30)
    weights = jnp.exp(scores - jnp.max(scores, axis=-1, keepdims=True))
    return weights * (1.0 / jnp.sum(weights, axis=-1, keepdims=True))


def spans(rows):
    out = []
    for row0 in range(0, rows, BLOCK):
        key0 = max(0, row0 - MAXLEN)
        out.append((row0, key0, row0 + BLOCK - key0))
    return out


def forward_kernel(
    q_ref, k_ref, v_ref, cos_ref, sin_ref, begin_ref, gq_ref, gk_ref,
    att_ref, query_ref, key_ref, value_ref,
):
    rows = q_ref.shape[0]
    cosine, sine = cos_ref[...], sin_ref[...]
    value_ref[...] = v_ref[...].astype(jnp.bfloat16)
    for kv in range(PAIR):
        key_ref[:, head(kv)] = normed_rotated(k_ref[:, head(kv)], gk_ref[...], cosine, sine)
    for h in range(PAIR * QUERY_GROUP):
        query_ref[:, head(h)] = normed_rotated(q_ref[:, head(h)], gq_ref[...], cosine, sine)
    for row0, key0, width in spans(rows):
        begin = begin_ref[pl.ds(row0, BLOCK), :]
        for h in range(PAIR * QUERY_GROUP):
            kv = h // QUERY_GROUP
            prob = probabilities(
                query_ref[pl.ds(row0, BLOCK), head(h)],
                key_ref[pl.ds(key0, width), head(kv)],
                begin, row0, key0,
            ).astype(jnp.bfloat16)
            att_ref[pl.ds(row0, BLOCK), head(h)] = matrix_product(
                prob, value_ref[pl.ds(key0, width), head(kv)]
            ).astype(jnp.bfloat16)


def backward_kernel(
    q_ref, k_ref, query_ref, key_ref, value_ref, da_ref, cos_ref, sin_ref, begin_ref,
    gq_ref, gk_ref,
    dq_ref, dk_ref, dv_ref, dgq_ref, dgk_ref,
    key_acc, value_acc,
):
    rows = q_ref.shape[0]
    scale = HEAD_SIZE ** -0.5
    key_acc[...] = jnp.zeros_like(key_acc)
    value_acc[...] = jnp.zeros_like(value_acc)
    total_q = jnp.zeros((1, HEAD_SIZE), jnp.float32)
    total_k = jnp.zeros((1, HEAD_SIZE), jnp.float32)
    for row0, key0, width in spans(rows):
        block, keys = pl.ds(row0, BLOCK), pl.ds(key0, width)
        begin = begin_ref[block, :]
        for h in range(PAIR * QUERY_GROUP):
            kv = h // QUERY_GROUP
            query, key = query_ref[block, head(h)], key_ref[keys, head(kv)]
            d_out = da_ref[block, head(h)]
            prob = probabilities(query, key, begin, row0, key0)
            d_prob = matmul_t(d_out, value_ref[keys, head(kv)])
            delta = jnp.sum(d_prob * prob, axis=-1, keepdims=True)
            d_scores = (prob * (d_prob - delta)).astype(jnp.bfloat16)
            d_query = matrix_product(d_scores, key) * scale
            key_acc[kv, keys, :] += inner_rows(d_scores, query)
            value_acc[kv, keys, :] += inner_rows(prob.astype(jnp.bfloat16), d_out)
            d_raw, d_gain = undo_norm(
                q_ref[block, head(h)], gq_ref[...], cos_ref[block, :], sin_ref[block, :], d_query
            )
            dq_ref[block, head(h)] = d_raw
            total_q = total_q + d_gain
    for kv in range(PAIR):
        d_raw, d_gain = undo_norm(
            k_ref[:, head(kv)], gk_ref[...], cos_ref[...], sin_ref[...], key_acc[kv] * scale
        )
        dk_ref[:, head(kv)] = d_raw
        dv_ref[:, head(kv)] = value_acc[kv].astype(jnp.bfloat16)
        total_k = total_k + d_gain
    dgq_ref[...] = total_q[None]
    dgk_ref[...] = total_k[None]


def attention_forward(qkv, cosine, sine, begin, gain_q, gain_k, kv_heads):
    rows = qkv.shape[0]
    wide, narrow = PAIR * QUERY_GROUP * HEAD_SIZE, PAIR * HEAD_SIZE
    pairs = kv_heads // PAIR
    whole = lambda a: pl.BlockSpec(a.shape, lambda g: (0,) * a.ndim)
    q_cols = kv_heads * QUERY_GROUP * HEAD_SIZE // narrow
    k_cols = kv_heads * HEAD_SIZE // narrow
    q_spec = pl.BlockSpec((rows, wide), lambda g: (0, g))
    n_spec = pl.BlockSpec((rows, narrow), lambda g: (0, g))
    bf = jnp.bfloat16
    return pl.pallas_call(
        forward_kernel,
        grid=(pairs,),
        in_specs=[
            q_spec,
            pl.BlockSpec((rows, narrow), lambda g: (0, q_cols + g)),
            pl.BlockSpec((rows, narrow), lambda g: (0, q_cols + k_cols + g)),
            whole(cosine), whole(sine), whole(begin), whole(gain_q), whole(gain_k),
        ],
        out_specs=[q_spec, q_spec, n_spec, n_spec],
        out_shape=[
            jax.ShapeDtypeStruct((rows, wide * pairs), bf),
            jax.ShapeDtypeStruct((rows, wide * pairs), bf),
            jax.ShapeDtypeStruct((rows, narrow * pairs), bf),
            jax.ShapeDtypeStruct((rows, narrow * pairs), bf),
        ],
        compiler_params=pltpu.CompilerParams(vmem_limit_bytes=VMEM),
        cost_estimate=pl.CostEstimate(flops=6 * 10**9, bytes_accessed=10**7, transcendentals=5 * 10**6),
        name="attention_forward",
    )(qkv, qkv, qkv, cosine, sine, begin, gain_q, gain_k)


def attention_backward(qkv, query, key, value, d_att, cosine, sine, begin, gain_q, gain_k, kv_heads):
    rows = qkv.shape[0]
    wide, narrow = PAIR * QUERY_GROUP * HEAD_SIZE, PAIR * HEAD_SIZE
    pairs = kv_heads // PAIR
    whole = lambda a: pl.BlockSpec(a.shape, lambda g: (0,) * a.ndim)
    q_cols = kv_heads * QUERY_GROUP * HEAD_SIZE // narrow
    q_spec = pl.BlockSpec((rows, wide), lambda g: (0, g))
    n_spec = pl.BlockSpec((rows, narrow), lambda g: (0, g))
    g_spec = pl.BlockSpec((1, 1, HEAD_SIZE), lambda g: (g, 0, 0))
    bf = jnp.bfloat16
    return pl.pallas_call(
        backward_kernel,
        grid=(pairs,),
        in_specs=[
            q_spec,
            pl.BlockSpec((rows, narrow), lambda g: (0, q_cols + g)),
            q_spec, n_spec, n_spec, q_spec,
            whole(cosine), whole(sine), whole(begin), whole(gain_q), whole(gain_k),
        ],
        out_specs=[q_spec, n_spec, n_spec, g_spec, g_spec],
        out_shape=[
            jax.ShapeDtypeStruct((rows, wide * pairs), bf),
            jax.ShapeDtypeStruct((rows, narrow * pairs), bf),
            jax.ShapeDtypeStruct((rows, narrow * pairs), bf),
            jax.ShapeDtypeStruct((pairs, 1, HEAD_SIZE), jnp.float32),
            jax.ShapeDtypeStruct((pairs, 1, HEAD_SIZE), jnp.float32),
        ],
        scratch_shapes=[
            pltpu.VMEM((PAIR, rows, HEAD_SIZE), jnp.float32),
            pltpu.VMEM((PAIR, rows, HEAD_SIZE), jnp.float32),
        ],
        compiler_params=pltpu.CompilerParams(vmem_limit_bytes=VMEM),
        cost_estimate=pl.CostEstimate(flops=2 * 10**10, bytes_accessed=10**7, transcendentals=5 * 10**6),
        name="attention_backward",
    )(qkv, qkv, query, key, value, d_att, cosine, sine, begin, gain_q, gain_k)


def pair_sum(value):
    return value + lax.ppermute(value, "tensor", [(0, 1), (1, 0)])


def local(
    tokens,
    lengths,
    w_query,
    key_weight,
    value_weight,
    w_output,
    w_gate,
    w_up,
    w_down,
    gain_attn,
    gain_ffn,
    gain_query,
    key_norm_gain,
    cotangent,
):
    bf, f32 = jnp.bfloat16, jnp.float32
    rows, width = tokens.shape
    part = w_query.shape[0]
    q_width, kv_width, ff = w_query.shape[1], key_weight.shape[1], w_gate.shape[1]
    kv_heads = kv_width // HEAD_SIZE
    qkv_width = q_width + 2 * kv_width

    gains = jnp.pad(jnp.stack([gain_attn, gain_ffn], axis=1), ((0, 0), (0, 126)))
    attn_pack = jnp.concatenate(
        [w_query, key_weight, value_weight, w_output.T, gains], axis=1
    )
    ffn_pack = jnp.concatenate([w_gate, w_up, w_down.T], axis=1)
    attn_all = lax.all_gather(attn_pack, "fsdp", axis=0, tiled=True)
    attn_all, ffn_pack = lax.optimization_barrier((attn_all, ffn_pack))
    ffn_all = lax.all_gather(ffn_pack, "fsdp", axis=0, tiled=True)
    qkv_all = attn_all[:, :qkv_width]
    output_t = attn_all[:, qkv_width : qkv_width + q_width]
    first_gain = attn_all[:, qkv_width + q_width].astype(f32)
    second_gain = attn_all[:, qkv_width + q_width + 1].astype(f32)
    query_gain = gain_query.astype(f32)[None]
    key_gain = key_norm_gain.astype(f32)[None]

    lens = lengths[0]
    ends = jnp.cumsum(lens)
    row_ids = jnp.arange(rows, dtype=jnp.int32)
    passed = row_ids[:, None] >= ends[None, :]
    begin = jnp.sum(jnp.where(passed, lens[None, :], 0), axis=1)
    position = (row_ids - begin).astype(f32)
    freq = THETA ** (-jnp.arange(HALF, dtype=f32) * 2.0 / HEAD_SIZE)
    angle = position[:, None] * freq[None, :]
    cosine, sine = jnp.cos(angle), jnp.sin(angle)
    cosine = jnp.concatenate([cosine, cosine], axis=1)
    sine = jnp.concatenate([-sine, sine], axis=1)
    begin = begin[:, None]

    x_float = tokens.astype(f32)
    h1 = root_mean_scale(x_float, first_gain).astype(bf)
    qkv = matrix_product(h1, qkv_all)
    attended, query, key, value = attention_forward(
        qkv, cosine, sine, begin, query_gain, key_gain, kv_heads
    )
    resid = x_float + pair_sum(matmul_t(attended, output_t))
    h2 = root_mean_scale(resid, second_gain).astype(bf)

    gate = matrix_product(h2, ffn_all[:, :ff])
    upward = matrix_product(h2, ffn_all[:, ff : 2 * ff])
    down_t = ffn_all[:, 2 * ff :]
    d_hidden = matrix_product(cotangent, down_t)
    hidden, pull_swish = jax.vjp(swish_product, gate, upward)
    d_gate, d_up = pull_swish(d_hidden)
    hidden = hidden.astype(bf)
    d_both = jnp.concatenate([d_gate.astype(bf), d_up.astype(bf)], axis=1)
    d_second = pair_sum(matmul_t(d_both, ffn_all[:, : 2 * ff]))
    grad_both = inner_rows(h2, d_both).astype(bf)
    grad_down = inner_rows(cotangent, hidden).astype(bf)
    ffn_grads = lax.psum_scatter(
        jnp.concatenate([grad_both, grad_down], axis=1), "fsdp", scatter_dimension=0, tiled=True
    )
    ffn_out = pair_sum(matmul_t(hidden, down_t).astype(bf)).astype(f32)
    layer_out = (resid + ffn_out).astype(bf)

    unused_norm, pull_second = jax.vjp(root_mean_scale, resid, second_gain)
    d_resid_norm, grad_second_gain = pull_second(d_second)
    d_resid = cotangent.astype(f32) + d_resid_norm
    d_branch = d_resid.astype(bf)
    d_attended = matrix_product(d_branch, output_t).astype(bf)
    d_q, d_k, d_v, gain_q_part, gain_k_part = attention_backward(
        qkv, query, key, value, d_attended, cosine, sine, begin, query_gain, key_gain, kv_heads
    )
    d_qkv = jnp.concatenate([d_q, d_k, d_v], axis=1)
    grad_qkv = inner_rows(h1, d_qkv).astype(bf)
    grad_out = inner_rows(d_branch, attended).astype(bf)
    attn_grads = lax.psum_scatter(
        jnp.concatenate([grad_qkv, grad_out], axis=1), "fsdp", scatter_dimension=0, tiled=True
    )
    d_first = pair_sum(matmul_t(d_qkv, qkv_all).astype(bf)).astype(f32)
    unused_first, pull_first = jax.vjp(root_mean_scale, x_float, first_gain)
    d_x_norm, grad_first_gain = pull_first(d_first)
    token_grad = (d_resid + d_x_norm).astype(bf)

    small = jnp.concatenate(
        [
            grad_first_gain * 0.5,
            grad_second_gain * 0.5,
            jnp.sum(gain_q_part, axis=(0, 1)),
            jnp.sum(gain_k_part, axis=(0, 1)),
        ]
    )
    small = lax.psum(small, ("fsdp", "tensor"))
    start = lax.axis_index("fsdp") * part
    shard_first = lax.dynamic_slice_in_dim(small, start, part, 0)
    shard_second = lax.dynamic_slice_in_dim(small, width + start, part, 0)
    gain_q_grad = small[2 * width : 2 * width + HEAD_SIZE]
    gain_k_grad = small[2 * width + HEAD_SIZE :]

    attn_grads = attn_grads.astype(f32)
    ffn_grads = ffn_grads.astype(f32)
    return (
        layer_out,
        token_grad,
        attn_grads[:, :q_width],
        attn_grads[:, q_width : q_width + kv_width],
        attn_grads[:, q_width + kv_width : qkv_width],
        attn_grads[:, qkv_width:].T,
        ffn_grads[:, :ff],
        ffn_grads[:, ff : 2 * ff],
        ffn_grads[:, 2 * ff :].T,
        shard_first,
        shard_second,
        gain_q_grad,
        gain_k_grad,
    )


def solution(mesh):
    return jax.shard_map(
        local,
        mesh=mesh,
        in_specs=(
            P("fsdp", None),
            P("fsdp", None),
            P("fsdp", "tensor"),
            P("fsdp", "tensor"),
            P("fsdp", "tensor"),
            P("tensor", "fsdp"),
            P("fsdp", "tensor"),
            P("fsdp", "tensor"),
            P("tensor", "fsdp"),
            P("fsdp"),
            P("fsdp"),
            P(),
            P(),
            P("fsdp", None),
        ),
        out_specs=(
            P("fsdp", None),
            P("fsdp", None),
            P("fsdp", "tensor"),
            P("fsdp", "tensor"),
            P("fsdp", "tensor"),
            P("tensor", "fsdp"),
            P("fsdp", "tensor"),
            P("fsdp", "tensor"),
            P("tensor", "fsdp"),
            P("fsdp"),
            P("fsdp"),
            P(),
            P(),
        ),
        check_vma=False,
    )
```

```python
import functools

import jax
import jax.numpy as jnp
from jax import lax
from jax.experimental import pallas as pl
from jax.experimental.pallas import tpu as pltpu
from jax.sharding import PartitionSpec as P

HEAD_SIZE = 64
HALF = 32
QUERY_GROUP = 2
BLOCK = 256
MAXLEN = 512
EPS = 1e-05
THETA = 1000000.0
PAIR = 2
VMEM = 60 * 1024 * 1024


def root_mean_scale(value, gain):
    return value * lax.rsqrt(jnp.mean(value * value, axis=-1, keepdims=True) + EPS) * gain


def swish_product(gate, upward):
    return gate * jax.nn.sigmoid(gate) * upward


def matrix_product(left, right):
    return jnp.dot(left, right, preferred_element_type=jnp.float32)


def matmul_t(left, right):
    return lax.dot_general(
        left, right, (((1,), (1,)), ((), ())), preferred_element_type=jnp.float32
    )


def inner_rows(left, right):
    return lax.dot_general(
        left, right, (((0,), (0,)), ((), ())), preferred_element_type=jnp.float32
    )


def swap_halves(value):
    return jnp.concatenate([value[:, HALF:], value[:, :HALF]], axis=1)


def head(index):
    return slice(index * HEAD_SIZE, (index + 1) * HEAD_SIZE)


def normed_rotated(raw, gain, cosine, sine):
    n = raw * lax.rsqrt(jnp.mean(raw * raw, axis=-1, keepdims=True) + EPS) * gain
    return (n * cosine + swap_halves(n) * sine).astype(jnp.bfloat16)


def undo_norm(raw, gain, cosine, sine, d_out):
    d_n = d_out * cosine - swap_halves(d_out) * sine
    r = lax.rsqrt(jnp.mean(raw * raw, axis=-1, keepdims=True) + EPS)
    scaled = raw * r
    d_gain = jnp.sum(d_n * scaled, axis=0, keepdims=True)
    g_d = gain * d_n
    d_raw = r * (g_d - scaled * jnp.mean(g_d * scaled, axis=-1, keepdims=True))
    return d_raw.astype(jnp.bfloat16), d_gain


def probabilities(query, key, begin, row0, key0):
    scores = matmul_t(query, key) * (HEAD_SIZE ** -0.5)
    rows = row0 + lax.broadcasted_iota(jnp.int32, scores.shape, 0)
    cols = key0 + lax.broadcasted_iota(jnp.int32, scores.shape, 1)
    allowed = (cols <= rows) & (cols >= begin)
    scores = jnp.where(allowed, scores, -1e30)
    weights = jnp.exp(scores - jnp.max(scores, axis=-1, keepdims=True))
    return weights * (1.0 / jnp.sum(weights, axis=-1, keepdims=True))


def spans(rows):
    out = []
    for row0 in range(0, rows, BLOCK):
        key0 = max(0, row0 - MAXLEN)
        out.append((row0, key0, row0 + BLOCK - key0))
    return out


def forward_kernel(
    q_ref, k_ref, v_ref, cos_ref, sin_ref, begin_ref, gq_ref, gk_ref,
    att_ref, query_ref, key_ref, value_ref,
):
    rows = q_ref.shape[0]
    cosine, sine = cos_ref[...], sin_ref[...]
    value_ref[...] = v_ref[...].astype(jnp.bfloat16)
    for kv in range(PAIR):
        key_ref[:, head(kv)] = normed_rotated(k_ref[:, head(kv)], gk_ref[...], cosine, sine)
    for h in range(PAIR * QUERY_GROUP):
        query_ref[:, head(h)] = normed_rotated(q_ref[:, head(h)], gq_ref[...], cosine, sine)
    for row0, key0, width in spans(rows):
        begin = begin_ref[pl.ds(row0, BLOCK), :]
        for h in range(PAIR * QUERY_GROUP):
            kv = h // QUERY_GROUP
            prob = probabilities(
                query_ref[pl.ds(row0, BLOCK), head(h)],
                key_ref[pl.ds(key0, width), head(kv)],
                begin, row0, key0,
            ).astype(jnp.bfloat16)
            att_ref[pl.ds(row0, BLOCK), head(h)] = matrix_product(
                prob, value_ref[pl.ds(key0, width), head(kv)]
            ).astype(jnp.bfloat16)


def backward_kernel(
    q_ref, k_ref, query_ref, key_ref, value_ref, da_ref, cos_ref, sin_ref, begin_ref,
    gq_ref, gk_ref,
    dq_ref, dk_ref, dv_ref, dgq_ref, dgk_ref,
    key_acc, value_acc,
):
    rows = q_ref.shape[0]
    scale = HEAD_SIZE ** -0.5
    key_acc[...] = jnp.zeros_like(key_acc)
    value_acc[...] = jnp.zeros_like(value_acc)
    total_q = jnp.zeros((1, HEAD_SIZE), jnp.float32)
    total_k = jnp.zeros((1, HEAD_SIZE), jnp.float32)
    for row0, key0, width in spans(rows):
        block, keys = pl.ds(row0, BLOCK), pl.ds(key0, width)
        begin = begin_ref[block, :]
        for h in range(PAIR * QUERY_GROUP):
            kv = h // QUERY_GROUP
            query, key = query_ref[block, head(h)], key_ref[keys, head(kv)]
            d_out = da_ref[block, head(h)]
            prob = probabilities(query, key, begin, row0, key0)
            d_prob = matmul_t(d_out, value_ref[keys, head(kv)])
            delta = jnp.sum(d_prob * prob, axis=-1, keepdims=True)
            d_scores = (prob * (d_prob - delta)).astype(jnp.bfloat16)
            d_query = matrix_product(d_scores, key) * scale
            key_acc[kv, keys, :] += inner_rows(d_scores, query)
            value_acc[kv, keys, :] += inner_rows(prob.astype(jnp.bfloat16), d_out)
            d_raw, d_gain = undo_norm(
                q_ref[block, head(h)], gq_ref[...], cos_ref[block, :], sin_ref[block, :], d_query
            )
            dq_ref[block, head(h)] = d_raw
            total_q = total_q + d_gain
    for kv in range(PAIR):
        d_raw, d_gain = undo_norm(
            k_ref[:, head(kv)], gk_ref[...], cos_ref[...], sin_ref[...], key_acc[kv] * scale
        )
        dk_ref[:, head(kv)] = d_raw
        dv_ref[:, head(kv)] = value_acc[kv].astype(jnp.bfloat16)
        total_k = total_k + d_gain
    dgq_ref[...] = total_q[None]
    dgk_ref[...] = total_k[None]


def attention_forward(qkv, cosine, sine, begin, gain_q, gain_k, kv_heads):
    rows = qkv.shape[0]
    wide, narrow = PAIR * QUERY_GROUP * HEAD_SIZE, PAIR * HEAD_SIZE
    pairs = kv_heads // PAIR
    whole = lambda a: pl.BlockSpec(a.shape, lambda g: (0,) * a.ndim)
    q_cols = kv_heads * QUERY_GROUP * HEAD_SIZE // narrow
    k_cols = kv_heads * HEAD_SIZE // narrow
    q_spec = pl.BlockSpec((rows, wide), lambda g: (0, g))
    n_spec = pl.BlockSpec((rows, narrow), lambda g: (0, g))
    bf = jnp.bfloat16
    return pl.pallas_call(
        forward_kernel,
        grid=(pairs,),
        in_specs=[
            q_spec,
            pl.BlockSpec((rows, narrow), lambda g: (0, q_cols + g)),
            pl.BlockSpec((rows, narrow), lambda g: (0, q_cols + k_cols + g)),
            whole(cosine), whole(sine), whole(begin), whole(gain_q), whole(gain_k),
        ],
        out_specs=[q_spec, q_spec, n_spec, n_spec],
        out_shape=[
            jax.ShapeDtypeStruct((rows, wide * pairs), bf),
            jax.ShapeDtypeStruct((rows, wide * pairs), bf),
            jax.ShapeDtypeStruct((rows, narrow * pairs), bf),
            jax.ShapeDtypeStruct((rows, narrow * pairs), bf),
        ],
        compiler_params=pltpu.CompilerParams(vmem_limit_bytes=VMEM),
        cost_estimate=pl.CostEstimate(flops=6 * 10**9, bytes_accessed=10**7, transcendentals=5 * 10**6),
        name="attention_forward",
    )(qkv, qkv, qkv, cosine, sine, begin, gain_q, gain_k)


def attention_backward(qkv, query, key, value, d_att, cosine, sine, begin, gain_q, gain_k, kv_heads):
    rows = qkv.shape[0]
    wide, narrow = PAIR * QUERY_GROUP * HEAD_SIZE, PAIR * HEAD_SIZE
    pairs = kv_heads // PAIR
    whole = lambda a: pl.BlockSpec(a.shape, lambda g: (0,) * a.ndim)
    q_cols = kv_heads * QUERY_GROUP * HEAD_SIZE // narrow
    q_spec = pl.BlockSpec((rows, wide), lambda g: (0, g))
    n_spec = pl.BlockSpec((rows, narrow), lambda g: (0, g))
    g_spec = pl.BlockSpec((1, 1, HEAD_SIZE), lambda g: (g, 0, 0))
    bf = jnp.bfloat16
    return pl.pallas_call(
        backward_kernel,
        grid=(pairs,),
        in_specs=[
            q_spec,
            pl.BlockSpec((rows, narrow), lambda g: (0, q_cols + g)),
            q_spec, n_spec, n_spec, q_spec,
            whole(cosine), whole(sine), whole(begin), whole(gain_q), whole(gain_k),
        ],
        out_specs=[q_spec, n_spec, n_spec, g_spec, g_spec],
        out_shape=[
            jax.ShapeDtypeStruct((rows, wide * pairs), bf),
            jax.ShapeDtypeStruct((rows, narrow * pairs), bf),
            jax.ShapeDtypeStruct((rows, narrow * pairs), bf),
            jax.ShapeDtypeStruct((pairs, 1, HEAD_SIZE), jnp.float32),
            jax.ShapeDtypeStruct((pairs, 1, HEAD_SIZE), jnp.float32),
        ],
        scratch_shapes=[
            pltpu.VMEM((PAIR, rows, HEAD_SIZE), jnp.float32),
            pltpu.VMEM((PAIR, rows, HEAD_SIZE), jnp.float32),
        ],
        compiler_params=pltpu.CompilerParams(vmem_limit_bytes=VMEM),
        cost_estimate=pl.CostEstimate(flops=2 * 10**10, bytes_accessed=10**7, transcendentals=5 * 10**6),
        name="attention_backward",
    )(qkv, qkv, query, key, value, d_att, cosine, sine, begin, gain_q, gain_k)


def pair_sum(value):
    return value + lax.ppermute(value, "tensor", [(0, 1), (1, 0)])


def local(
    tokens,
    lengths,
    w_query,
    key_weight,
    value_weight,
    w_output,
    w_gate,
    w_up,
    w_down,
    gain_attn,
    gain_ffn,
    gain_query,
    key_norm_gain,
    cotangent,
):
    bf, f32 = jnp.bfloat16, jnp.float32
    rows, width = tokens.shape
    part = w_query.shape[0]
    q_width, kv_width, ff = w_query.shape[1], key_weight.shape[1], w_gate.shape[1]
    kv_heads = kv_width // HEAD_SIZE
    qkv_width = q_width + 2 * kv_width

    gains = jnp.pad(jnp.stack([gain_attn, gain_ffn], axis=1), ((0, 0), (0, 126)))
    attn_pack = jnp.concatenate(
        [w_query, key_weight, value_weight, w_output.T, gains], axis=1
    )
    ffn_pack = jnp.concatenate([w_gate, w_up, w_down.T], axis=1)
    attn_all = lax.all_gather(attn_pack, "fsdp", axis=0, tiled=True)
    attn_all, ffn_pack = lax.optimization_barrier((attn_all, ffn_pack))
    ffn_all = lax.all_gather(ffn_pack, "fsdp", axis=0, tiled=True)
    qkv_all = attn_all[:, :qkv_width]
    output_t = attn_all[:, qkv_width : qkv_width + q_width]
    first_gain = attn_all[:, qkv_width + q_width].astype(f32)
    second_gain = attn_all[:, qkv_width + q_width + 1].astype(f32)
    query_gain = gain_query.astype(f32)[None]
    key_gain = key_norm_gain.astype(f32)[None]

    lens = lengths[0]
    ends = jnp.cumsum(lens)
    row_ids = jnp.arange(rows, dtype=jnp.int32)
    passed = row_ids[:, None] >= ends[None, :]
    begin = jnp.sum(jnp.where(passed, lens[None, :], 0), axis=1)
    position = (row_ids - begin).astype(f32)
    freq = THETA ** (-jnp.arange(HALF, dtype=f32) * 2.0 / HEAD_SIZE)
    angle = position[:, None] * freq[None, :]
    cosine, sine = jnp.cos(angle), jnp.sin(angle)
    cosine = jnp.concatenate([cosine, cosine], axis=1)
    sine = jnp.concatenate([-sine, sine], axis=1)
    begin = begin[:, None]

    x_float = tokens.astype(f32)
    h1 = root_mean_scale(x_float, first_gain).astype(bf)
    qkv = matrix_product(h1, qkv_all)
    attended, query, key, value = attention_forward(
        qkv, cosine, sine, begin, query_gain, key_gain, kv_heads
    )
    resid = x_float + pair_sum(matmul_t(attended, output_t))
    h2 = root_mean_scale(resid, second_gain).astype(bf)

    gate = matrix_product(h2, ffn_all[:, :ff])
    upward = matrix_product(h2, ffn_all[:, ff : 2 * ff])
    down_t = ffn_all[:, 2 * ff :]
    d_hidden = matrix_product(cotangent, down_t)
    hidden, pull_swish = jax.vjp(swish_product, gate, upward)
    d_gate, d_up = pull_swish(d_hidden)
    hidden = hidden.astype(bf)
    d_both = jnp.concatenate([d_gate.astype(bf), d_up.astype(bf)], axis=1)
    d_second = pair_sum(matmul_t(d_both, ffn_all[:, : 2 * ff]))
    grad_both = inner_rows(h2, d_both).astype(bf)
    grad_down = inner_rows(cotangent, hidden).astype(bf)
    ffn_packed = jnp.concatenate([grad_both, grad_down], axis=1)
    ffn_packed, d_second = lax.optimization_barrier((ffn_packed, d_second))
    ffn_grads = lax.psum_scatter(ffn_packed, "fsdp", scatter_dimension=0, tiled=True)
    ffn_out = pair_sum(matmul_t(hidden, down_t).astype(bf)).astype(f32)
    layer_out = (resid + ffn_out).astype(bf)

    unused_norm, pull_second = jax.vjp(root_mean_scale, resid, second_gain)
    d_resid_norm, grad_second_gain = pull_second(d_second)
    d_resid = cotangent.astype(f32) + d_resid_norm
    d_branch = d_resid.astype(bf)
    d_attended = matrix_product(d_branch, output_t).astype(bf)
    d_q, d_k, d_v, gain_q_part, gain_k_part = attention_backward(
        qkv, query, key, value, d_attended, cosine, sine, begin, query_gain, key_gain, kv_heads
    )
    d_qkv = jnp.concatenate([d_q, d_k, d_v], axis=1)
    grad_qkv = inner_rows(h1, d_qkv).astype(bf)
    grad_out = inner_rows(d_branch, attended).astype(bf)
    attn_packed = jnp.concatenate([grad_qkv, grad_out], axis=1)
    attn_packed, ffn_grads = lax.optimization_barrier((attn_packed, ffn_grads))
    attn_grads = lax.psum_scatter(attn_packed, "fsdp", scatter_dimension=0, tiled=True)
    d_first = pair_sum(matmul_t(d_qkv, qkv_all).astype(bf)).astype(f32)
    unused_first, pull_first = jax.vjp(root_mean_scale, x_float, first_gain)
    d_x_norm, grad_first_gain = pull_first(d_first)
    token_grad = (d_resid + d_x_norm).astype(bf)

    small = jnp.concatenate(
        [
            grad_first_gain * 0.5,
            grad_second_gain * 0.5,
            jnp.sum(gain_q_part, axis=(0, 1)),
            jnp.sum(gain_k_part, axis=(0, 1)),
        ]
    )
    small = lax.psum(small, ("fsdp", "tensor"))
    start = lax.axis_index("fsdp") * part
    shard_first = lax.dynamic_slice_in_dim(small, start, part, 0)
    shard_second = lax.dynamic_slice_in_dim(small, width + start, part, 0)
    gain_q_grad = small[2 * width : 2 * width + HEAD_SIZE]
    gain_k_grad = small[2 * width + HEAD_SIZE :]

    attn_grads = attn_grads.astype(f32)
    ffn_grads = ffn_grads.astype(f32)
    return (
        layer_out,
        token_grad,
        attn_grads[:, :q_width],
        attn_grads[:, q_width : q_width + kv_width],
        attn_grads[:, q_width + kv_width : qkv_width],
        attn_grads[:, qkv_width:].T,
        ffn_grads[:, :ff],
        ffn_grads[:, ff : 2 * ff],
        ffn_grads[:, 2 * ff :].T,
        shard_first,
        shard_second,
        gain_q_grad,
        gain_k_grad,
    )


def solution(mesh):
    return jax.shard_map(
        local,
        mesh=mesh,
        in_specs=(
            P("fsdp", None),
            P("fsdp", None),
            P("fsdp", "tensor"),
            P("fsdp", "tensor"),
            P("fsdp", "tensor"),
            P("tensor", "fsdp"),
            P("fsdp", "tensor"),
            P("fsdp", "tensor"),
            P("tensor", "fsdp"),
            P("fsdp"),
            P("fsdp"),
            P(),
            P(),
            P("fsdp", None),
        ),
        out_specs=(
            P("fsdp", None),
            P("fsdp", None),
            P("fsdp", "tensor"),
            P("fsdp", "tensor"),
            P("fsdp", "tensor"),
            P("tensor", "fsdp"),
            P("fsdp", "tensor"),
            P("fsdp", "tensor"),
            P("tensor", "fsdp"),
            P("fsdp"),
            P("fsdp"),
            P(),
            P(),
        ),
        check_vma=False,
    )
```
